32 devices in a mesh: gx: 4 (over x, core), gy: 4 (over z), ta: 2 (over y).
Axes of the slice: x: 2, y: 2, z: 4, core: 2. Of those that a mesh axis runs over, the one named last changes fastest.
Arguments:
- tokens: bfloat16 [4, 4, 4, 128, 512], P('gx', 'gy', 'ta'), may hold values from -6 to 6
- validity: int32 [4, 4, 4, 128], P('gx', 'gy', 'ta'), may hold values 0 or 1
- tile_counts: int32 [4, 4], replicated, may hold values from 16 to 128, as said below
- neighbours: int32 [4, 4, 9], P('gx', 'gy'), may hold values from 0 to 1, as said below
- mask_token: bfloat16 [512], replicated, may hold values from -4 to 4
- norm_gains: float32 [3, 512], replicated, may hold values from 0.25 to 1.75
- agent_qkv: bfloat16 [512, 1536], replicated, may hold values from -3 to 3
- agent_out: bfloat16 [512, 512], replicated, may hold values from -0.25 to 0.25
- time_qkv: bfloat16 [512, 1536], replicated, may hold values from -3 to 3
- time_out: bfloat16 [512, 512], replicated, may hold values from -0.25 to 0.25
- widen_weight: bfloat16 [512, 2048], replicated, may hold values from -0.25 to 0.25
- narrow_weight: bfloat16 [2048, 512], replicated, may hold values from -0.125 to 0.125
Outputs:
- layer_out: bfloat16 [4, 4, 4, 128, 512], P('gx', 'gy', 'ta')
The draws below stay inside these ranges and needn't reach their ends.
Inputs may be any that keep to these rules, and one draw needn't show every extreme that they name: Tile i, j has its live agents in slots 0 to tile_counts[i, j] - 1; some tile is full. `neighbours`: entry 3 (di + 1) + (dj + 1) is 1 when the tile attends to the tile at offset di, dj; the centre entry is always 1. `validity`: 1 marks an observed agent step.
All inputs are finite; a program needn't handle non-finite values. No bound on the sum of `validity` on one device may be relied on, other than what follows from the above.
Results may differ from the reference program's by a relative error of at most 0.015.
Values may be sent and summed in bfloat16 or wider, within the bound.
A program may use at most 128 MiB of HBM per device.

```python
from functools import partial
import jax
import jax.numpy as jnp
from jax import lax

D = 512
HEADS = 8
HEAD_DIM = 64
FF = 2048
A_DEV = 128
NTX = 4
NTY = 4
T_SIZE = 4


def draw_tile_counts(key, part):
    drawn_counts = jax.random.randint(jax.random.fold_in(key, 11), (NTX * NTY,), A_DEV // 8, A_DEV + 1)
    chosen_tile = jax.random.randint(jax.random.fold_in(key, 12), (), 0, NTX * NTY)
    flat_counts = jnp.where(jnp.arange(NTX * NTY) == chosen_tile, A_DEV, drawn_counts)
    return flat_counts.reshape(NTX, NTY).astype(jnp.int32)


def draw_neighbours(key, part):
    drawn_bits = jax.random.randint(jax.random.fold_in(key, 13), (NTX, NTY, 9), 0, 4)
    flags = (drawn_bits > 0).astype(jnp.int32)
    return flags.at[:, :, 4].set(1).astype(jnp.int32)


def projection_draw(key):
    spread_scale = D ** (-0.5)
    drawn = jax.random.truncated_normal(jax.random.fold_in(key, 1), -3.0, 3.0, (D, 3 * D), jnp.float32) * spread_scale
    return jnp.clip(drawn, -3.0, 3.0)


def draw_agent_qkv(key, part):
    return projection_draw(jax.random.fold_in(key, 21)).astype(jnp.bfloat16)


def draw_time_qkv(key, part):
    return projection_draw(jax.random.fold_in(key, 22)).astype(jnp.bfloat16)


def plant(values, stream_key, low, high):
    shape = values.shape
    index_at = [jax.random.randint(jax.random.fold_in(stream_key, axis), (), 0, shape[axis]) for axis in range(len(shape))]
    values = values.at[tuple(index_at)].set(low)
    longest = shape.index(max(shape))
    index_at[longest] = (index_at[longest] + 1) % shape[longest]
    return values.at[tuple(index_at)].set(high)


def block_scale(rng, dims, cuts, smallest, high):
    factor_of = 1.0
    for position, blocks in cuts:
        steps = jax.random.uniform(jax.random.fold_in(jax.random.fold_in(rng, 6), position), (blocks,), jnp.float32, smallest / len(cuts), high / len(cuts))
        factor_of = factor_of * jnp.repeat(jnp.exp(steps), dims[position] // blocks).reshape((-1,) + (1,) * (len(dims) - 1 - position))
    return factor_of


def noise(key, dims, scale, reach, cuts=(), kind=jnp.bfloat16):
    entries = scale * jax.random.normal(key, dims, jnp.float32)
    if cuts:
        entries = entries * block_scale(key, dims, cuts, -0.22, 0.18)
    return jnp.clip(entries, -reach, reach).astype(kind)


def setup_inputs(seed: int = 0) -> dict:
    arg_keys = jax.random.split(jax.random.key(seed), 13)
    tokens = noise(arg_keys[0], (NTX, NTY, T_SIZE, A_DEV, D), 1.0, 6.0, ((0, 4), (1, 4), (2, 2)))
    validity = plant((jax.random.randint(arg_keys[1], (NTX, NTY, T_SIZE, A_DEV), 0, 4) < 3).astype(jnp.int32), jax.random.fold_in(arg_keys[1], 1), 0, 1)
    tile_counts = draw_tile_counts(jax.random.fold_in(arg_keys[12], 71), 0)
    neighbours = draw_neighbours(jax.random.fold_in(arg_keys[12], 71), 0)
    mask_token = noise(arg_keys[4], (D,), 1.0, 4.0)
    norm_gains = jnp.clip(1.0 + 0.15 * jax.random.normal(arg_keys[5], (3, D), jnp.float32), 0.25, 1.75)
    agent_qkv = draw_agent_qkv(jax.random.fold_in(arg_keys[12], 71), 0)
    agent_out = noise(arg_keys[7], (D, D), D ** -0.5, 0.25)
    time_qkv = draw_time_qkv(jax.random.fold_in(arg_keys[12], 71), 0)
    time_out = noise(arg_keys[9], (D, D), D ** -0.5, 0.25)
    widen_weight = noise(arg_keys[10], (D, FF), D ** -0.5, 0.25)
    narrow_weight = noise(arg_keys[11], (FF, D), FF ** -0.5, 0.125)
    return {"tokens": tokens, "validity": validity, "tile_counts": tile_counts, "neighbours": neighbours, "mask_token": mask_token, "norm_gains": norm_gains, "agent_qkv": agent_qkv, "agent_out": agent_out, "time_qkv": time_qkv, "time_out": time_out, "widen_weight": widen_weight, "narrow_weight": narrow_weight}


EPSILON = 1e-05
NEGATIVE = -1e+30

def layer_norm(values, gain_row):
    values = values.astype(jnp.float32)
    center = values - lax.optimization_barrier(jnp.mean(values, axis=-1, keepdims=True))
    spread = lax.optimization_barrier(jnp.mean(center * center, axis=-1, keepdims=True))
    return (center * lax.rsqrt(spread + EPSILON) * gain_row).astype(jnp.bfloat16)

def project(values, weight):
    return jnp.dot(values, weight, preferred_element_type=jnp.float32)

def agent_attention(queries, padded_kv, padded_live, neighbour_flags, tile_index):
    tile_index = tile_index.astype(jnp.int32)
    tile_row = (tile_index // NTY).astype(jnp.int32)
    column = (tile_index % NTY).astype(jnp.int32)
    zero = jnp.zeros((), jnp.int32)
    near_block = lax.dynamic_slice(padded_kv, (tile_row, column, zero, zero, zero), (3, 3, T_SIZE, A_DEV, 2 * D))
    near_live = lax.dynamic_slice(padded_live, (tile_row, column, zero), (3, 3, A_DEV))
    chosen = neighbour_flags[tile_index].reshape(3, 3) == 1
    key_live = (near_live & chosen[:, :, None]).reshape(9 * A_DEV)
    own_queries = queries[tile_index].astype(jnp.float32).reshape(T_SIZE, A_DEV, HEADS, HEAD_DIM)
    key_rows = near_block[..., :D].astype(jnp.float32).reshape(3, 3, T_SIZE, A_DEV, HEADS, HEAD_DIM)
    value_rows = near_block[..., D:].astype(jnp.float32).reshape(3, 3, T_SIZE, A_DEV, HEADS, HEAD_DIM)
    value_rows = value_rows.transpose(2, 0, 1, 3, 4, 5).reshape(T_SIZE, 9 * A_DEV, HEADS, HEAD_DIM)
    scores = jnp.einsum('tqhd,xytkhd->thqxyk', own_queries, key_rows).reshape(T_SIZE, HEADS, A_DEV, 9 * A_DEV)
    scores = scores * HEAD_DIM ** (-0.5)
    scores = jnp.where(key_live, scores, NEGATIVE)
    row_max = lax.optimization_barrier(jnp.max(scores, axis=-1, keepdims=True))
    weights = jnp.exp(scores - row_max)
    weights = (weights / lax.optimization_barrier(jnp.sum(weights, axis=-1, keepdims=True))).astype(jnp.bfloat16)
    weights = lax.optimization_barrier(weights).astype(jnp.float32)
    attended = jnp.einsum('thqn,tnhd->tqhd', weights, value_rows)
    return attended.reshape(T_SIZE, A_DEV, D).astype(jnp.bfloat16)

def time_attention(exchanged):
    own_queries = exchanged[..., :D].astype(jnp.float32).reshape(T_SIZE, A_DEV, HEADS, HEAD_DIM)
    key_rows = exchanged[..., D:2 * D].astype(jnp.float32).reshape(T_SIZE, A_DEV, HEADS, HEAD_DIM)
    value_rows = exchanged[..., 2 * D:].astype(jnp.float32).reshape(T_SIZE, A_DEV, HEADS, HEAD_DIM)
    scores = jnp.einsum('qahd,kahd->ahqk', own_queries, key_rows) * HEAD_DIM ** (-0.5)
    row_max = lax.optimization_barrier(jnp.max(scores, axis=-1, keepdims=True))
    weights = jnp.exp(scores - row_max)
    weights = weights / lax.optimization_barrier(jnp.sum(weights, axis=-1, keepdims=True))
    attended = jnp.einsum('ahqk,kahd->qahd', weights, value_rows, precision=lax.Precision.HIGHEST)
    return attended.reshape(T_SIZE, A_DEV, D).astype(jnp.bfloat16)

def reference(tokens, validity, tile_counts, neighbours, mask_token, norm_gains, agent_qkv, agent_out, time_qkv, time_out, widen_weight, narrow_weight):
    masked_input = jnp.where(validity[..., None] == 1, tokens, mask_token)
    normed = layer_norm(masked_input, norm_gains[0])
    packed = project(normed, agent_qkv).astype(jnp.bfloat16)
    queries = packed[..., :D].reshape(NTX * NTY, T_SIZE, A_DEV, D)
    padded_kv = jnp.pad(packed[..., D:], ((1, 1), (1, 1), (0, 0), (0, 0), (0, 0)))
    slot_ids = jnp.arange(A_DEV, dtype=jnp.int32)
    slot_live = slot_ids[None, None, :] < tile_counts[:, :, None]
    padded_live = jnp.pad(slot_live, ((1, 1), (1, 1), (0, 0)))
    neighbour_flags = neighbours.reshape(NTX * NTY, 9)
    tile_list = jnp.arange(NTX * NTY, dtype=jnp.int32)
    attended = lax.map(partial(agent_attention, queries, padded_kv, padded_live, neighbour_flags), tile_list)
    attended = attended.reshape(NTX, NTY, T_SIZE, A_DEV, D)
    after_agents = (masked_input.astype(jnp.float32) + project(attended, agent_out)).astype(jnp.bfloat16)
    normed = layer_norm(after_agents, norm_gains[1])
    packed = project(normed, time_qkv).astype(jnp.bfloat16).reshape(NTX * NTY, T_SIZE, A_DEV, 3 * D)
    attended = lax.map(time_attention, packed).reshape(NTX, NTY, T_SIZE, A_DEV, D)
    after_time = (after_agents.astype(jnp.float32) + project(attended, time_out)).astype(jnp.bfloat16)
    normed = layer_norm(after_time, norm_gains[2])
    hidden = jnp.maximum(project(normed, widen_weight), 0.0).astype(jnp.bfloat16)
    return (after_time.astype(jnp.float32) + project(hidden, narrow_weight)).astype(jnp.bfloat16)
```

```python
import functools

import jax
import jax.numpy as jnp
from jax import lax
from jax.experimental import pallas as pl
from jax.experimental.pallas import tpu as pltpu
from jax.sharding import PartitionSpec as P

HEADS = 8
EPSILON = 1e-05
NEGATIVE = -1e30
F32 = jnp.float32
BF16 = jnp.bfloat16
MESH = pl.DeviceIdType.MESH

OFFSETS = ((0, 0), (-1, 0), (1, 0), (0, -1), (0, 1), (-1, -1), (1, -1), (-1, 1), (1, 1))


def layer_norm(values, gain_row):
    values = values.astype(F32)
    center = values - jnp.mean(values, axis=-1, keepdims=True)
    spread = jnp.mean(center * center, axis=-1, keepdims=True)
    return (center * lax.rsqrt(spread + EPSILON) * gain_row).astype(BF16)


def dot(a, b):
    return jnp.dot(a, b, preferred_element_type=F32)


def dot_t(a, b):
    return lax.dot_general(a, b, (((1,), (1,)), ((), ())), preferred_element_type=F32)


def kernel(
    sizes,
    tokens,
    validity,
    counts,
    flags,
    mask_token,
    gains,
    *rest,
):
    nx, ny, nt = sizes
    weights_hbm = rest[:6]
    out = rest[6]
    weights = rest[7:13]
    (tok, near, masked, query, kv, after, steps, tq, tkv, tmix) = rest[13:23]
    (load_sem, send_sem, recv_sem, tsend_sem, trecv_sem) = rest[23:]
    moments, slots, width = tok.shape
    head_dim = width // HEADS
    scale = head_dim**-0.5
    gx, gy, ta = lax.axis_index("gx"), lax.axis_index("gy"), lax.axis_index("ta")
    has = {-1: gx > 0, 1: gx < nx - 1}
    hasy = {-1: gy > 0, 1: gy < ny - 1}

    def load(i, src, dst):
        return pltpu.make_async_copy(src, dst, load_sem.at[i])

    loads = [load(0, tokens, tok)] + [
        load(i + 1, s, d) for i, (s, d) in enumerate(zip(weights_hbm, weights))
    ]
    for item in loads:
        item.start()

    barrier = pltpu.get_barrier_semaphore()
    for d in (-1, 1):

        @pl.when(has[d])
        def _():
            pl.semaphore_signal(barrier, inc=1, device_id=(gx + d, gy, ta), device_id_type=MESH)

        @pl.when(hasy[d])
        def _():
            pl.semaphore_signal(barrier, inc=1, device_id=(gx, gy + d, ta), device_id_type=MESH)

    for k in range(1, nt):
        pl.semaphore_signal(
            barrier, inc=1, device_id=(gx, gy, lax.rem(ta + k, nt)), device_id_type=MESH
        )

    for index, (di, dj) in enumerate(OFFSETS):
        inside = None
        for d, table in ((di, has), (dj, hasy)):
            if d:
                inside = table[d] if inside is None else jnp.logical_and(inside, table[d])
        if inside is not None:

            @pl.when(jnp.logical_not(inside))
            def _():
                near[index] = jnp.zeros(near.shape[1:], BF16)

    def along_y(m, d):
        dst = OFFSETS.index((0, -d))
        return pltpu.make_async_remote_copy(
            near.at[0, m], near.at[dst, m], send_sem.at[dst, m], recv_sem.at[dst, m],
            device_id=(gx, gy + d, ta), device_id_type=MESH,
        )

    def along_x(m, d, dj):
        src, dst = OFFSETS.index((0, dj)), OFFSETS.index((-d, dj))
        return pltpu.make_async_remote_copy(
            near.at[src, m], near.at[dst, m], send_sem.at[dst, m], recv_sem.at[dst, m],
            device_id=(gx + d, gy, ta), device_id_type=MESH,
        )

    def along_t(m, k):
        return pltpu.make_async_remote_copy(
            steps.at[m], steps.at[k * moments + m], tsend_sem.at[k - 1, m], trecv_sem.at[k - 1, m],
            device_id=(gx, gy, lax.rem(ta + k, nt)), device_id_type=MESH,
        )

    loads[0].wait()
    greeted = (nt - 1) + sum(
        jnp.where(c, 1, 0).astype(jnp.int32) for c in (has[-1], has[1], hasy[-1], hasy[1])
    )
    for m in range(moments):
        seen = jnp.broadcast_to(validity[m : m + 1, :].astype(F32), (128, slots)).T
        seen = jnp.concatenate([seen] * (width // 128), axis=1) == 1.0
        x = jnp.where(seen, tok[m].astype(F32), mask_token[...].astype(F32))
        masked[m] = x.astype(BF16)
        near[0, m] = layer_norm(x, gains[0:1, :])
        if m == 0:
            pl.semaphore_wait(barrier, greeted)
        for d in (-1, 1):

            @pl.when(hasy[d])
            def _():
                along_y(m, d).start()

        for d in (-1, 1):

            @pl.when(has[d])
            def _():
                along_x(m, d, 0).start()

    qkv_w, out_w, tqkv_w, tout_w, widen_w, narrow_w = weights
    loads[1].wait()
    own = near[0].reshape(moments * slots, width)
    query[...] = (dot(own, qkv_w[:, :width]) * scale).astype(BF16).reshape(query.shape)
    own_kv = dot(own, qkv_w[:, width:]).astype(BF16)
    for m in range(moments):
        kv[m, :slots] = own_kv[m * slots : (m + 1) * slots]

    def project_near(m, first, last):
        rows = near[first:last, m].reshape((last - first) * slots, width)
        kv[m, first * slots : last * slots] = dot(rows, qkv_w[:, width:]).astype(BF16)

    for m in range(moments):
        for dj in (-1, 1):

            @pl.when(hasy[dj])
            def _():
                along_y(m, -dj).wait_recv()
                for d in (-1, 1):

                    @pl.when(has[d])
                    def _():
                        along_x(m, d, dj).start()

        for d in (-1, 1):

            @pl.when(has[d])
            def _():
                along_x(m, -d, 0).wait_recv()

        project_near(m, 1, 5)

    lane = lax.broadcasted_iota(jnp.int32, (1, slots), 1)
    live = []
    for di, dj in OFFSETS:
        i, j = gx + di, gy + dj
        inside = jnp.logical_and(
            jnp.logical_and(i >= 0, i < nx), jnp.logical_and(j >= 0, j < ny)
        )
        count = counts[jnp.clip(i, 0, nx - 1), jnp.clip(j, 0, ny - 1)]
        chosen = flags[0, 3 * (di + 1) + (dj + 1)] == 1
        limit = jnp.where(jnp.logical_and(inside, chosen), count, 0)
        live.append(jnp.where(lane < limit, 0.0, 1.0))
    live = jnp.concatenate(live, axis=1) == 0.0

    group = 256
    heads_in = group // head_dim
    head_of = lax.broadcasted_iota(jnp.int32, (slots, group), 1) // head_dim

    loads[2].wait()
    for m in range(moments):
        for d in (-1, 1):
            for dj in (-1, 1):

                @pl.when(jnp.logical_and(has[d], hasy[dj]))
                def _():
                    along_x(m, -d, dj).wait_recv()

        project_near(m, 5, 9)
        parts = []
        for g in range(width // group):
            q = query[m, :, g * group : (g + 1) * group]
            stacked = jnp.concatenate(
                [jnp.where(head_of == h, q, jnp.zeros_like(q)) for h in range(heads_in)], axis=0
            )
            keys = kv[m, :, g * group : (g + 1) * group]
            values = kv[m, :, width + g * group : width + (g + 1) * group]
            scores = jnp.where(live, dot_t(stacked, keys), NEGATIVE)
            top = jnp.max(scores, axis=-1, keepdims=True)
            soft = jnp.exp(scores - top)
            total = jnp.sum(soft, axis=-1, keepdims=True)
            mixed = dot(soft.astype(BF16), values) * (1.0 / total)
            part = mixed[:slots]
            for h in range(1, heads_in):
                part = jnp.where(head_of == h, mixed[h * slots : (h + 1) * slots], part)
            parts.append(part.astype(BF16))
        mix = jnp.concatenate(parts, axis=1)
        result = (masked[m].astype(F32) + dot(mix, out_w[...])).astype(BF16)
        after[m] = result
        steps[m] = layer_norm(result, gains[1:2, :])
        for k in range(1, nt):
            along_t(m, k).start()

    loads[3].wait()
    rows = steps[:moments].reshape(moments * slots, width)
    tq[...] = (dot(rows, tqkv_w[:, :width]) * scale).astype(BF16).reshape(tq.shape)
    tkv[:moments] = (
        dot(rows, tqkv_w[:, width:]).astype(BF16).reshape(moments, slots, 2 * width)
    )
    for k in range(1, nt):
        for m in range(moments):
            along_t(m, k).wait_recv()
        rows = steps[k * moments : (k + 1) * moments].reshape(moments * slots, width)
        tkv[k * moments : (k + 1) * moments] = (
            dot(rows, tqkv_w[:, width:]).astype(BF16).reshape(moments, slots, 2 * width)
        )

    total_steps = nt * moments
    same = (
        lax.broadcasted_iota(jnp.int32, (group, group), 0) // head_dim
        == lax.broadcasted_iota(jnp.int32, (group, group), 1) // head_dim
    )
    ones = jnp.where(same, 1.0, 0.0).astype(BF16)
    piece = max(16, min(slots, 512 // total_steps))

    def time_piece(start):
        at = pl.ds(start, piece)
        for m in range(moments):
            for g in range(width // group):
                cols = slice(g * group, (g + 1) * group)
                q = tq[m, at, cols].astype(F32)
                keys = tkv[:, at, cols].astype(F32)
                prod = (q[None] * keys).reshape(total_steps * piece, group)
                high = prod.astype(BF16)
                low = (prod - high.astype(F32)).astype(BF16)
                scores = (dot(high, ones) + dot(low, ones)).reshape(total_steps, piece, group)
                soft = jnp.exp(scores - jnp.max(scores, axis=0)[None])
                total = jnp.sum(soft, axis=0)
                values = tkv[:, at, width + g * group : width + (g + 1) * group].astype(F32)
                mixed = jnp.sum(soft * values, axis=0) / total
                tmix[m, at, cols] = mixed.astype(BF16)

    if piece == slots:
        time_piece(0)
    else:

        def body(i, carry):
            time_piece(pl.multiple_of(i * piece, piece))
            return carry

        lax.fori_loop(0, slots // piece, body, 0)

    loads[4].wait()
    rows = moments * slots
    after_time = (
        after[...].reshape(rows, width).astype(F32)
        + dot(tmix[...].reshape(rows, width), tout_w[...])
    ).astype(BF16)
    normed = layer_norm(after_time, gains[2:3, :])
    loads[5].wait()
    hidden = jnp.maximum(dot(normed, widen_w[...]), 0.0).astype(BF16)
    loads[6].wait()
    out[...] = (
        (after_time.astype(F32) + dot(hidden, narrow_w[...])).astype(BF16).reshape(out.shape)
    )

    for m in range(moments):
        for d in (-1, 1):

            @pl.when(hasy[d])
            def _():
                along_y(m, d).wait_send()

            @pl.when(has[d])
            def _():
                along_x(m, d, 0).wait_send()

            for dj in (-1, 1):

                @pl.when(jnp.logical_and(has[d], hasy[dj]))
                def _():
                    along_x(m, d, dj).wait_send()

        for k in range(1, nt):
            along_t(m, k).wait_send()


def per_device(sizes, tokens, validity, tile_counts, neighbours, mask_token, norm_gains, *weights):
    moments, slots, width = tokens.shape[2:]
    steps = moments * sizes[2]
    vmem = pl.BlockSpec(memory_space=pltpu.VMEM)
    smem = pl.BlockSpec(memory_space=pltpu.SMEM)
    anywhere = pl.BlockSpec(memory_space=pl.ANY)
    result = pl.pallas_call(
        functools.partial(kernel, sizes),
        out_shape=jax.ShapeDtypeStruct((moments, slots, width), BF16),
        in_specs=[anywhere, vmem, smem, smem, vmem, vmem] + [anywhere] * 6,
        out_specs=vmem,
        scratch_shapes=[pltpu.VMEM(w.shape, BF16) for w in weights]
        + [
            pltpu.VMEM((moments, slots, width), BF16),
            pltpu.VMEM((9, moments, slots, width), BF16),
            pltpu.VMEM((moments, slots, width), BF16),
            pltpu.VMEM((moments, slots, width), BF16),
            pltpu.VMEM((moments, 9 * slots, 2 * width), BF16),
            pltpu.VMEM((moments, slots, width), BF16),
            pltpu.VMEM((steps, slots, width), BF16),
            pltpu.VMEM((moments, slots, width), BF16),
            pltpu.VMEM((steps, slots, 2 * width), BF16),
            pltpu.VMEM((moments, slots, width), BF16),
            pltpu.SemaphoreType.DMA((7,)),
            pltpu.SemaphoreType.DMA((9, moments)),
            pltpu.SemaphoreType.DMA((9, moments)),
            pltpu.SemaphoreType.DMA((max(sizes[2] - 1, 1), moments)),
            pltpu.SemaphoreType.DMA((max(sizes[2] - 1, 1), moments)),
        ],
        compiler_params=pltpu.CompilerParams(
            collective_id=0, has_side_effects=True, vmem_limit_bytes=56 * 1024 * 1024
        ),
    )(
        tokens[0, 0],
        validity[0, 0],
        tile_counts,
        neighbours[0],
        mask_token[None],
        norm_gains,
        *weights,
    )
    return result[None, None]


def solution(mesh):
    sizes = tuple(mesh.shape[name] for name in ("gx", "gy", "ta"))
    in_specs = (
        P("gx", "gy", "ta", None, None),
        P("gx", "gy", "ta", None),
        P(),
        P("gx", "gy", None),
    ) + (P(),) * 8
    return jax.shard_map(
        functools.partial(per_device, sizes),
        mesh=mesh,
        in_specs=in_specs,
        out_specs=P("gx", "gy", "ta", None, None),
        check_vma=False,
    )
```

```python
import functools

import jax
import jax.numpy as jnp
from jax import lax
from jax.experimental import pallas as pl
from jax.experimental.pallas import tpu as pltpu
from jax.sharding import PartitionSpec as P

HEADS = 8
EPSILON = 1e-05
NEGATIVE = -1e30
F32 = jnp.float32
BF16 = jnp.bfloat16
MESH = pl.DeviceIdType.MESH

OFFSETS = ((0, 0), (-1, 0), (1, 0), (0, -1), (0, 1), (-1, -1), (1, -1), (-1, 1), (1, 1))


def layer_norm(values, gain_row):
    values = values.astype(F32)
    center = values - jnp.mean(values, axis=-1, keepdims=True)
    spread = jnp.mean(center * center, axis=-1, keepdims=True)
    return (center * lax.rsqrt(spread + EPSILON) * gain_row).astype(BF16)


def dot(a, b):
    return jnp.dot(a, b, preferred_element_type=F32)


def dot_t(a, b):
    return lax.dot_general(a, b, (((1,), (1,)), ((), ())), preferred_element_type=F32)


def kernel(
    sizes,
    tokens,
    validity,
    counts,
    flags,
    mask_token,
    gains,
    *rest,
):
    nx, ny, nt = sizes
    weights_hbm = rest[:6]
    out = rest[6]
    weights = rest[7:13]
    (tok, near, masked, query, kv, after, steps, tq, tkv, tmix, held) = rest[13:24]
    (load_sem, send_sem, recv_sem, tsend_sem, trecv_sem) = rest[24:]
    moments, slots, width = tok.shape
    head_dim = width // HEADS
    scale = head_dim**-0.5
    gx, gy, ta = lax.axis_index("gx"), lax.axis_index("gy"), lax.axis_index("ta")
    has = {-1: gx > 0, 1: gx < nx - 1}
    hasy = {-1: gy > 0, 1: gy < ny - 1}

    def load(i, src, dst):
        return pltpu.make_async_copy(src, dst, load_sem.at[i])

    loads = [load(0, tokens, tok)] + [
        load(i + 1, s, d) for i, (s, d) in enumerate(zip(weights_hbm, weights))
    ]
    for item in loads:
        item.start()

    barrier = pltpu.get_barrier_semaphore()
    for d in (-1, 1):

        @pl.when(has[d])
        def _():
            pl.semaphore_signal(barrier, inc=1, device_id=(gx + d, gy, ta), device_id_type=MESH)

        @pl.when(hasy[d])
        def _():
            pl.semaphore_signal(barrier, inc=1, device_id=(gx, gy + d, ta), device_id_type=MESH)

    for k in range(1, nt):
        pl.semaphore_signal(
            barrier, inc=1, device_id=(gx, gy, lax.rem(ta + k, nt)), device_id_type=MESH
        )

    for index, (di, dj) in enumerate(OFFSETS):
        inside = None
        for d, table in ((di, has), (dj, hasy)):
            if d:
                inside = table[d] if inside is None else jnp.logical_and(inside, table[d])
        if inside is not None:

            @pl.when(jnp.logical_not(inside))
            def _():
                near[index] = jnp.zeros(near.shape[1:], BF16)

    def along_y(m, d):
        dst = OFFSETS.index((0, -d))
        return pltpu.make_async_remote_copy(
            near.at[0, m], near.at[dst, m], send_sem.at[dst, m], recv_sem.at[dst, m],
            device_id=(gx, gy + d, ta), device_id_type=MESH,
        )

    def along_x(m, d, dj):
        src, dst = OFFSETS.index((0, dj)), OFFSETS.index((-d, dj))
        return pltpu.make_async_remote_copy(
            near.at[src, m], near.at[dst, m], send_sem.at[dst, m], recv_sem.at[dst, m],
            device_id=(gx + d, gy, ta), device_id_type=MESH,
        )

    def along_t(m, k):
        return pltpu.make_async_remote_copy(
            steps.at[m], steps.at[k * moments + m], tsend_sem.at[k - 1, m], trecv_sem.at[k - 1, m],
            device_id=(gx, gy, lax.rem(ta + k, nt)), device_id_type=MESH,
        )

    hidden_token = mask_token[...].astype(F32)[None, :]
    loads[0].wait()
    greeted = (nt - 1) + sum(
        jnp.where(c, 1, 0).astype(jnp.int32) for c in (has[-1], has[1], hasy[-1], hasy[1])
    )
    for m in range(moments):
        seen = jnp.broadcast_to(validity[m : m + 1, :].astype(F32), (128, slots)).T
        seen = jnp.concatenate([seen] * (width // 128), axis=1) == 1.0
        x = jnp.where(seen, tok[m].astype(F32), hidden_token)
        masked[m] = x.astype(BF16)
        near[0, m] = layer_norm(x, gains[0:1, :])
        if m == 0:
            pl.semaphore_wait(barrier, greeted)
        for d in (-1, 1):

            @pl.when(hasy[d])
            def _():
                along_y(m, d).start()

        for d in (-1, 1):

            @pl.when(has[d])
            def _():
                along_x(m, d, 0).start()

    qkv_w, out_w, tqkv_w, tout_w, widen_w, narrow_w = weights
    loads[1].wait()
    own = near[0].reshape(moments * slots, width)
    query[...] = (dot(own, qkv_w[:, :width]) * scale).astype(BF16).reshape(query.shape)
    own_kv = dot(own, qkv_w[:, width:]).astype(BF16)
    for m in range(moments):
        kv[m, :slots] = own_kv[m * slots : (m + 1) * slots]

    def project_near(m, first, last):
        rows = near[first:last, m].reshape((last - first) * slots, width)
        kv[m, first * slots : last * slots] = dot(rows, qkv_w[:, width:]).astype(BF16)

    lane = lax.broadcasted_iota(jnp.int32, (1, slots), 1)
    live = []
    for di, dj in OFFSETS:
        i, j = gx + di, gy + dj
        inside = jnp.logical_and(
            jnp.logical_and(i >= 0, i < nx), jnp.logical_and(j >= 0, j < ny)
        )
        count = counts[jnp.clip(i, 0, nx - 1), jnp.clip(j, 0, ny - 1)]
        chosen = flags[0, 3 * (di + 1) + (dj + 1)] == 1
        limit = jnp.where(jnp.logical_and(inside, chosen), count, 0)
        live.append(jnp.where(lane < limit, 0.0, 1.0))
    live = jnp.concatenate(live, axis=1) == 0.0

    group = 256
    heads_in = group // head_dim
    head_of = lax.broadcasted_iota(jnp.int32, (slots, group), 1) // head_dim


    def merge(first, second):
        acc_a, top_a, sum_a = first
        acc_b, top_b, sum_b = second
        top = jnp.maximum(top_a, top_b)
        a, b = jnp.exp(top_a - top), jnp.exp(top_b - top)
        return acc_a * a + acc_b * b, top, sum_a * a + sum_b * b

    def attend(m, first, last):
        parts = []
        span = slice(first * slots, last * slots)
        for g in range(width // group):
            q = query[m, :, g * group : (g + 1) * group]
            stacked = jnp.concatenate(
                [jnp.where(head_of == h, q, jnp.zeros_like(q)) for h in range(heads_in)], axis=0
            )
            keys = kv[m, span, g * group : (g + 1) * group]
            values = kv[m, span, width + g * group : width + (g + 1) * group]
            scores = jnp.where(live[:, span], dot_t(stacked, keys), NEGATIVE)
            top = jnp.max(scores, axis=-1, keepdims=True)
            soft = jnp.exp(scores - top)
            total = jnp.sum(soft, axis=-1, keepdims=True)
            mixed = dot(soft.astype(BF16), values)

            def pick(rows):
                part = jnp.broadcast_to(rows[:slots], (slots, group))
                for h in range(1, heads_in):
                    part = jnp.where(head_of == h, rows[h * slots : (h + 1) * slots], part)
                return part

            parts.append([pick(mixed), pick(top), pick(total)])
        return [jnp.concatenate(p, axis=1) for p in zip(*parts)]

    def keep(m, state):
        for n in range(3):
            held[m, n] = state[n]

    def kept(m):
        return [held[m, n] for n in range(3)]

    def first_part(m):
        keep(m, attend(m, 0, 3))

    def second_part(m):
        project_near(m, 3, 5)
        keep(m, merge(kept(m), attend(m, 3, 5)))

    for m in range(moments):
        for d in (-1, 1):

            @pl.when(has[d])
            def _():
                along_x(m, -d, 0).wait_recv()

        project_near(m, 1, 3)
        for dj in (-1, 1):

            @pl.when(hasy[dj])
            def _():
                along_y(m, -dj).wait_recv()
                for d in (-1, 1):

                    @pl.when(has[d])
                    def _():
                        along_x(m, d, dj).start()

        if m > 0:
            second_part(m - 1)
        first_part(m)
    second_part(moments - 1)

    loads[2].wait()
    for m in range(moments):
        for d in (-1, 1):
            for dj in (-1, 1):

                @pl.when(jnp.logical_and(has[d], hasy[dj]))
                def _():
                    along_x(m, -d, dj).wait_recv()

        project_near(m, 5, 9)
        acc, _, total = merge(kept(m), attend(m, 5, 9))
        mix = (acc / total).astype(BF16)
        result = (masked[m].astype(F32) + dot(mix, out_w[...])).astype(BF16)
        after[m] = result
        steps[m] = layer_norm(result, gains[1:2, :])
        for k in range(1, nt):
            along_t(m, k).start()

    loads[3].wait()
    rows = steps[:moments].reshape(moments * slots, width)
    tq[...] = (dot(rows, tqkv_w[:, :width]) * scale).astype(BF16).reshape(tq.shape)
    tkv[:moments] = (
        dot(rows, tqkv_w[:, width:]).astype(BF16).reshape(moments, slots, 2 * width)
    )
    for m in range(moments):
        for k in range(1, nt):
            along_t(m, k).wait_recv()
            tkv[k * moments + m] = dot(steps[k * moments + m], tqkv_w[:, width:]).astype(BF16)

    total_steps = nt * moments
    same = (
        lax.broadcasted_iota(jnp.int32, (group, group), 0) // head_dim
        == lax.broadcasted_iota(jnp.int32, (group, group), 1) // head_dim
    )
    ones = jnp.where(same, 1.0, 0.0).astype(BF16)
    piece = max(16, min(slots, 512 // total_steps))

    def time_piece(start):
        at = pl.ds(start, piece)
        for m in range(moments):
            for g in range(width // group):
                cols = slice(g * group, (g + 1) * group)
                q = tq[m, at, cols].astype(F32)
                keys = tkv[:, at, cols].astype(F32)
                prod = (q[None] * keys).reshape(total_steps * piece, group)
                high = prod.astype(BF16)
                low = (prod - high.astype(F32)).astype(BF16)
                scores = (dot(high, ones) + dot(low, ones)).reshape(total_steps, piece, group)
                soft = jnp.exp(scores - jnp.max(scores, axis=0)[None])
                total = jnp.sum(soft, axis=0)
                values = tkv[:, at, width + g * group : width + (g + 1) * group].astype(F32)
                mixed = jnp.sum(soft * values, axis=0) / total
                tmix[m, at, cols] = mixed.astype(BF16)

    if piece == slots:
        time_piece(0)
    else:

        def body(i, carry):
            time_piece(pl.multiple_of(i * piece, piece))
            return carry

        lax.fori_loop(0, slots // piece, body, 0)

    loads[4].wait()
    rows = moments * slots
    after_time = (
        after[...].reshape(rows, width).astype(F32)
        + dot(tmix[...].reshape(rows, width), tout_w[...])
    ).astype(BF16)
    normed = layer_norm(after_time, gains[2:3, :])
    loads[5].wait()
    hidden = jnp.maximum(dot(normed, widen_w[...]), 0.0).astype(BF16)
    loads[6].wait()
    out[...] = (
        (after_time.astype(F32) + dot(hidden, narrow_w[...])).astype(BF16).reshape(out.shape)
    )

    for m in range(moments):
        for d in (-1, 1):

            @pl.when(hasy[d])
            def _():
                along_y(m, d).wait_send()

            @pl.when(has[d])
            def _():
                along_x(m, d, 0).wait_send()

            for dj in (-1, 1):

                @pl.when(jnp.logical_and(has[d], hasy[dj]))
                def _():
                    along_x(m, d, dj).wait_send()

        for k in range(1, nt):
            along_t(m, k).wait_send()


def per_device(sizes, tokens, validity, tile_counts, neighbours, mask_token, norm_gains, *weights):
    moments, slots, width = tokens.shape[2:]
    steps = moments * sizes[2]
    vmem = pl.BlockSpec(memory_space=pltpu.VMEM)
    smem = pl.BlockSpec(memory_space=pltpu.SMEM)
    anywhere = pl.BlockSpec(memory_space=pl.ANY)
    result = pl.pallas_call(
        functools.partial(kernel, sizes),
        out_shape=jax.ShapeDtypeStruct((moments, slots, width), BF16),
        in_specs=[anywhere, vmem, smem, smem, vmem, vmem] + [anywhere] * 6,
        out_specs=vmem,
        scratch_shapes=[pltpu.VMEM(w.shape, BF16) for w in weights]
        + [
            pltpu.VMEM((moments, slots, width), BF16),
            pltpu.VMEM((9, moments, slots, width), BF16),
            pltpu.VMEM((moments, slots, width), BF16),
            pltpu.VMEM((moments, slots, width), BF16),
            pltpu.VMEM((moments, 9 * slots, 2 * width), BF16),
            pltpu.VMEM((moments, slots, width), BF16),
            pltpu.VMEM((steps, slots, width), BF16),
            pltpu.VMEM((moments, slots, width), BF16),
            pltpu.VMEM((steps, slots, 2 * width), BF16),
            pltpu.VMEM((moments, slots, width), BF16),
            pltpu.VMEM((moments, 3, slots, width), F32),
            pltpu.SemaphoreType.DMA((7,)),
            pltpu.SemaphoreType.DMA((9, moments)),
            pltpu.SemaphoreType.DMA((9, moments)),
            pltpu.SemaphoreType.DMA((max(sizes[2] - 1, 1), moments)),
            pltpu.SemaphoreType.DMA((max(sizes[2] - 1, 1), moments)),
        ],
        compiler_params=pltpu.CompilerParams(
            collective_id=0, has_side_effects=True, vmem_limit_bytes=56 * 1024 * 1024
        ),
    )(
        tokens[0, 0],
        validity[0, 0],
        tile_counts,
        neighbours[0],
        mask_token,
        norm_gains,
        *weights,
    )
    return result[None, None]


def solution(mesh):
    sizes = tuple(mesh.shape[name] for name in ("gx", "gy", "ta"))
    in_specs = (
        P("gx", "gy", "ta", None, None),
        P("gx", "gy", "ta", None),
        P(),
        P("gx", "gy", None),
    ) + (P(),) * 8
    return jax.shard_map(
        functools.partial(per_device, sizes),
        mesh=mesh,
        in_specs=in_specs,
        out_specs=P("gx", "gy", "ta", None, None),
        check_vma=False,
    )
```

```python
import functools

import jax
import jax.numpy as jnp
from jax import lax
from jax.experimental import pallas as pl
from jax.experimental.pallas import tpu as pltpu
from jax.sharding import PartitionSpec as P

HEADS = 8
EPSILON = 1e-05
NEGATIVE = -1e30
CUTS = 2
F32 = jnp.float32
BF16 = jnp.bfloat16
MESH = pl.DeviceIdType.MESH

OFFSETS = ((0, 0), (-1, 0), (1, 0), (0, -1), (0, 1), (-1, -1), (1, -1), (-1, 1), (1, 1))


def layer_norm(values, gain_row):
    values = values.astype(F32)
    center = values - jnp.mean(values, axis=-1, keepdims=True)
    spread = jnp.mean(center * center, axis=-1, keepdims=True)
    return (center * lax.rsqrt(spread + EPSILON) * gain_row).astype(BF16)


def dot(a, b):
    return jnp.dot(a, b, preferred_element_type=F32)


def dot_t(a, b):
    return lax.dot_general(a, b, (((1,), (1,)), ((), ())), preferred_element_type=F32)


def kernel(
    sizes,
    tokens,
    validity,
    counts,
    flags,
    mask_token,
    gains,
    *rest,
):
    nx, ny, nt = sizes
    weights_hbm = rest[:6]
    out = rest[6]
    weights = rest[7:13]
    (tok, near, masked, query, kv, after, steps, tq, tkv, tmix, held) = rest[13:24]
    (load_sem, send_sem, recv_sem, tsend_sem, trecv_sem) = rest[24:]
    moments, slots, width = tok.shape
    head_dim = width // HEADS
    scale = head_dim**-0.5
    cuts = CUTS
    gx, gy, ta = lax.axis_index("gx"), lax.axis_index("gy"), lax.axis_index("ta")
    has = {-1: gx > 0, 1: gx < nx - 1}
    hasy = {-1: gy > 0, 1: gy < ny - 1}

    def load(i, src, dst):
        return pltpu.make_async_copy(src, dst, load_sem.at[i])

    loads = [load(0, tokens, tok)] + [
        load(i + 1, s, d) for i, (s, d) in enumerate(zip(weights_hbm, weights))
    ]
    for item in loads:
        item.start()

    barrier = pltpu.get_barrier_semaphore()
    for d in (-1, 1):

        @pl.when(has[d])
        def _():
            pl.semaphore_signal(barrier, inc=1, device_id=(gx + d, gy, ta), device_id_type=MESH)

        @pl.when(hasy[d])
        def _():
            pl.semaphore_signal(barrier, inc=1, device_id=(gx, gy + d, ta), device_id_type=MESH)

    for k in range(1, nt):
        pl.semaphore_signal(
            barrier, inc=1, device_id=(gx, gy, lax.rem(ta + k, nt)), device_id_type=MESH
        )

    for index, (di, dj) in enumerate(OFFSETS):
        inside = None
        for d, table in ((di, has), (dj, hasy)):
            if d:
                inside = table[d] if inside is None else jnp.logical_and(inside, table[d])
        if inside is not None:

            @pl.when(jnp.logical_not(inside))
            def _():
                near[index] = jnp.zeros(near.shape[1:], BF16)

    def along_y(m, d):
        dst = OFFSETS.index((0, -d))
        return pltpu.make_async_remote_copy(
            near.at[0, m], near.at[dst, m], send_sem.at[dst, m], recv_sem.at[dst, m],
            device_id=(gx, gy + d, ta), device_id_type=MESH,
        )

    def along_x(m, d, dj):
        src, dst = OFFSETS.index((0, dj)), OFFSETS.index((-d, dj))
        return pltpu.make_async_remote_copy(
            near.at[src, m], near.at[dst, m], send_sem.at[dst, m], recv_sem.at[dst, m],
            device_id=(gx + d, gy, ta), device_id_type=MESH,
        )

    def along_t(m, k, c):
        at = pl.ds(c * slots // cuts, slots // cuts)
        return pltpu.make_async_remote_copy(
            steps.at[m, at], steps.at[k * moments + m, at],
            tsend_sem.at[k - 1, m * cuts + c], trecv_sem.at[k - 1, m * cuts + c],
            device_id=(gx, gy, lax.rem(ta + k, nt)), device_id_type=MESH,
        )

    hidden_token = mask_token[...].astype(F32)[None, :]
    loads[0].wait()
    greeted = (nt - 1) + sum(
        jnp.where(c, 1, 0).astype(jnp.int32) for c in (has[-1], has[1], hasy[-1], hasy[1])
    )
    for m in range(moments):
        seen = jnp.broadcast_to(validity[m : m + 1, :].astype(F32), (128, slots)).T
        seen = jnp.concatenate([seen] * (width // 128), axis=1) == 1.0
        x = jnp.where(seen, tok[m].astype(F32), hidden_token)
        masked[m] = x.astype(BF16)
        near[0, m] = layer_norm(x, gains[0:1, :])
        if m == 0:
            pl.semaphore_wait(barrier, greeted)
        for d in (-1, 1):

            @pl.when(hasy[d])
            def _():
                along_y(m, d).start()

        for d in (-1, 1):

            @pl.when(has[d])
            def _():
                along_x(m, d, 0).start()

    qkv_w, out_w, tqkv_w, tout_w, widen_w, narrow_w = weights
    loads[1].wait()
    own = near[0].reshape(moments * slots, width)
    query[...] = (dot(own, qkv_w[:, :width]) * scale).astype(BF16).reshape(query.shape)
    own_kv = dot(own, qkv_w[:, width:]).astype(BF16)
    for m in range(moments):
        kv[m, :slots] = own_kv[m * slots : (m + 1) * slots]

    def project_near(m, first, last):
        rows = near[first:last, m].reshape((last - first) * slots, width)
        kv[m, first * slots : last * slots] = dot(rows, qkv_w[:, width:]).astype(BF16)

    lane = lax.broadcasted_iota(jnp.int32, (1, slots), 1)
    live = []
    for di, dj in OFFSETS:
        i, j = gx + di, gy + dj
        inside = jnp.logical_and(
            jnp.logical_and(i >= 0, i < nx), jnp.logical_and(j >= 0, j < ny)
        )
        count = counts[jnp.clip(i, 0, nx - 1), jnp.clip(j, 0, ny - 1)]
        chosen = flags[0, 3 * (di + 1) + (dj + 1)] == 1
        limit = jnp.where(jnp.logical_and(inside, chosen), count, 0)
        live.append(jnp.where(lane < limit, 0.0, 1.0))
    live = jnp.concatenate(live, axis=1) == 0.0

    group = 256
    heads_in = group // head_dim
    head_of = lax.broadcasted_iota(jnp.int32, (slots, group), 1) // head_dim


    def merge(first, second):
        acc_a, top_a, sum_a = first
        acc_b, top_b, sum_b = second
        top = jnp.maximum(top_a, top_b)
        a, b = jnp.exp(top_a - top), jnp.exp(top_b - top)
        return acc_a * a + acc_b * b, top, sum_a * a + sum_b * b

    def attend(m, first, last, low=0, high=None):
        high = slots if high is None else high
        count = high - low
        lanes = head_of[:count]
        parts = []
        span = slice(first * slots, last * slots)
        for g in range(width // group):
            q = query[m, low:high, g * group : (g + 1) * group]
            stacked = jnp.concatenate(
                [jnp.where(lanes == h, q, jnp.zeros_like(q)) for h in range(heads_in)], axis=0
            )
            keys = kv[m, span, g * group : (g + 1) * group]
            values = kv[m, span, width + g * group : width + (g + 1) * group]
            scores = jnp.where(live[:, span], dot_t(stacked, keys), NEGATIVE)
            top = jnp.max(scores, axis=-1, keepdims=True)
            soft = jnp.exp(scores - top)
            total = jnp.sum(soft, axis=-1, keepdims=True)
            mixed = dot(soft.astype(BF16), values)

            def pick(rows):
                part = jnp.broadcast_to(rows[:count], (count, group))
                for h in range(1, heads_in):
                    part = jnp.where(lanes == h, rows[h * count : (h + 1) * count], part)
                return part

            parts.append([pick(mixed), pick(top), pick(total)])
        return [jnp.concatenate(p, axis=1) for p in zip(*parts)]

    def keep(m, state):
        for n in range(3):
            held[m, n] = state[n]

    def kept(m):
        return [held[m, n] for n in range(3)]

    def first_part(m):
        keep(m, attend(m, 0, 3))

    def second_part(m):
        project_near(m, 3, 5)
        keep(m, merge(kept(m), attend(m, 3, 5)))

    for m in range(moments):
        for d in (-1, 1):

            @pl.when(has[d])
            def _():
                along_x(m, -d, 0).wait_recv()

        project_near(m, 1, 3)
        if m == 0:
            first_part(m)
        for dj in (-1, 1):

            @pl.when(hasy[dj])
            def _():
                along_y(m, -dj).wait_recv()
                for d in (-1, 1):

                    @pl.when(has[d])
                    def _():
                        along_x(m, d, dj).start()

        if m > 0:
            second_part(m - 1)
            first_part(m)
    second_part(moments - 1)

    loads[2].wait()
    for m in range(moments):
        for d in (-1, 1):
            for dj in (-1, 1):

                @pl.when(jnp.logical_and(has[d], hasy[dj]))
                def _():
                    along_x(m, -d, dj).wait_recv()

        project_near(m, 5, 9)
        for c in range(cuts):
            at = slice(c * slots // cuts, (c + 1) * slots // cuts)
            state = [held[m, n, at] for n in range(3)]
            acc, _, total = merge(state, attend(m, 5, 9, at.start, at.stop))
            mix = (acc / total).astype(BF16)
            result = (masked[m, at].astype(F32) + dot(mix, out_w[...])).astype(BF16)
            after[m, at] = result
            steps[m, at] = layer_norm(result, gains[1:2, :])
            for k in range(1, nt):
                along_t(m, k, c).start()

    loads[3].wait()
    rows = steps[:moments].reshape(moments * slots, width)
    tq[...] = (dot(rows, tqkv_w[:, :width]) * scale).astype(BF16).reshape(tq.shape)
    tkv[:moments] = (
        dot(rows, tqkv_w[:, width:]).astype(BF16).reshape(moments, slots, 2 * width)
    )
    for m in range(moments):
        for k in range(1, nt):
            for c in range(cuts):
                along_t(m, k, c).wait_recv()
            tkv[k * moments + m] = dot(steps[k * moments + m], tqkv_w[:, width:]).astype(BF16)

    total_steps = nt * moments
    same = (
        lax.broadcasted_iota(jnp.int32, (group, group), 0) // head_dim
        == lax.broadcasted_iota(jnp.int32, (group, group), 1) // head_dim
    )
    ones = jnp.where(same, 1.0, 0.0).astype(BF16)
    piece = max(16, min(slots, 512 // total_steps))

    def time_piece(start):
        at = pl.ds(start, piece)
        for m in range(moments):
            for g in range(width // group):
                cols = slice(g * group, (g + 1) * group)
                q = tq[m, at, cols].astype(F32)
                keys = tkv[:, at, cols].astype(F32)
                prod = (q[None] * keys).reshape(total_steps * piece, group)
                high = prod.astype(BF16)
                low = (prod - high.astype(F32)).astype(BF16)
                scores = (dot(high, ones) + dot(low, ones)).reshape(total_steps, piece, group)
                soft = jnp.exp(scores - jnp.max(scores, axis=0)[None])
                total = jnp.sum(soft, axis=0)
                values = tkv[:, at, width + g * group : width + (g + 1) * group].astype(F32)
                mixed = jnp.sum(soft * values, axis=0) / total
                tmix[m, at, cols] = mixed.astype(BF16)

    if piece == slots:
        time_piece(0)
    else:

        def body(i, carry):
            time_piece(pl.multiple_of(i * piece, piece))
            return carry

        lax.fori_loop(0, slots // piece, body, 0)

    loads[4].wait()
    rows = moments * slots
    after_time = (
        after[...].reshape(rows, width).astype(F32)
        + dot(tmix[...].reshape(rows, width), tout_w[...])
    ).astype(BF16)
    normed = layer_norm(after_time, gains[2:3, :])
    loads[5].wait()
    hidden = jnp.maximum(dot(normed, widen_w[...]), 0.0).astype(BF16)
    loads[6].wait()
    out[...] = (
        (after_time.astype(F32) + dot(hidden, narrow_w[...])).astype(BF16).reshape(out.shape)
    )

    for m in range(moments):
        for d in (-1, 1):

            @pl.when(hasy[d])
            def _():
                along_y(m, d).wait_send()

            @pl.when(has[d])
            def _():
                along_x(m, d, 0).wait_send()

            for dj in (-1, 1):

                @pl.when(jnp.logical_and(has[d], hasy[dj]))
                def _():
                    along_x(m, d, dj).wait_send()

        for k in range(1, nt):
            for c in range(cuts):
                along_t(m, k, c).wait_send()


def per_device(sizes, tokens, validity, tile_counts, neighbours, mask_token, norm_gains, *weights):
    moments, slots, width = tokens.shape[2:]
    steps = moments * sizes[2]
    vmem = pl.BlockSpec(memory_space=pltpu.VMEM)
    smem = pl.BlockSpec(memory_space=pltpu.SMEM)
    anywhere = pl.BlockSpec(memory_space=pl.ANY)
    result = pl.pallas_call(
        functools.partial(kernel, sizes),
        out_shape=jax.ShapeDtypeStruct((moments, slots, width), BF16),
        in_specs=[anywhere, vmem, smem, smem, vmem, vmem] + [anywhere] * 6,
        out_specs=vmem,
        scratch_shapes=[pltpu.VMEM(w.shape, BF16) for w in weights]
        + [
            pltpu.VMEM((moments, slots, width), BF16),
            pltpu.VMEM((9, moments, slots, width), BF16),
            pltpu.VMEM((moments, slots, width), BF16),
            pltpu.VMEM((moments, slots, width), BF16),
            pltpu.VMEM((moments, 9 * slots, 2 * width), BF16),
            pltpu.VMEM((moments, slots, width), BF16),
            pltpu.VMEM((steps, slots, width), BF16),
            pltpu.VMEM((moments, slots, width), BF16),
            pltpu.VMEM((steps, slots, 2 * width), BF16),
            pltpu.VMEM((moments, slots, width), BF16),
            pltpu.VMEM((moments, 3, slots, width), F32),
            pltpu.SemaphoreType.DMA((7,)),
            pltpu.SemaphoreType.DMA((9, moments)),
            pltpu.SemaphoreType.DMA((9, moments)),
            pltpu.SemaphoreType.DMA((max(sizes[2] - 1, 1), moments * CUTS)),
            pltpu.SemaphoreType.DMA((max(sizes[2] - 1, 1), moments * CUTS)),
        ],
        compiler_params=pltpu.CompilerParams(
            collective_id=0, has_side_effects=True, vmem_limit_bytes=56 * 1024 * 1024
        ),
    )(
        tokens[0, 0],
        validity[0, 0],
        tile_counts,
        neighbours[0],
        mask_token,
        norm_gains,
        *weights,
    )
    return result[None, None]


def solution(mesh):
    sizes = tuple(mesh.shape[name] for name in ("gx", "gy", "ta"))
    in_specs = (
        P("gx", "gy", "ta", None, None),
        P("gx", "gy", "ta", None),
        P(),
        P("gx", "gy", None),
    ) + (P(),) * 8
    return jax.shard_map(
        functools.partial(per_device, sizes),
        mesh=mesh,
        in_specs=in_specs,
        out_specs=P("gx", "gy", "ta", None, None),
        check_vma=False,
    )
```
